512 devices in a mesh: dp: 64 (over z, y), mp: 8 (over x, core).
Axes of the slice: x: 4, y: 8, z: 8, core: 2. Of those that a mesh axis runs over, the one named last changes fastest.
Arguments:
- activations: bfloat16 [57344, 384], P('dp'), may hold values from -24 to 24
- cotangents: bfloat16 [57344, 18432], P('dp', 'mp'), may hold values from -24 to 24
- row_second: float32 [384], P('dp'), may hold values from 0.003 to 0.3
- column_second: float32 [18432], P('mp'), may hold values from 0.003 to 0.3
Outputs:
- update: float32 [384, 18432], P('dp', 'mp')
- row_moment: float32 [384], P('dp')
- column_moment: float32 [18432], P('mp')
The draws below stay inside these ranges and needn't reach their ends.
All inputs are finite; a program needn't handle non-finite values.
Results may differ from the reference program's by a relative error of at most 0.00075.
Values sent between devices are 32-bit elements; how exact they have to be, the bound alone decides.
A program may use at most 64 MiB of HBM per device.

```python
import math
import jax
import jax.numpy as jnp
from jax import lax

N = 18432
ROWS = 384
TOKENS = 57344


def column_scales(key, count):
    spread = 0.1 * jnp.exp(jnp.log(10.0) * jax.random.uniform(key, (count,), jnp.float32))
    rising = jnp.exp(jnp.log(3.0) * jnp.arange(count, dtype=jnp.float32) / count)
    return spread * rising


def draw_activations(key, part):
    key = jax.random.fold_in(key, 11)
    key_scale, key_noise = jax.random.split(key, 2)
    scales = column_scales(key_scale, ROWS)
    values = jax.random.normal(key_noise, (TOKENS, ROWS), jnp.float32)
    return (values * scales).astype(jnp.bfloat16)


def draw_cotangents(key, part):
    key = jax.random.fold_in(key, 23)
    key_scale, key_noise = jax.random.split(key, 2)
    scales = column_scales(key_scale, N)
    values = jax.random.normal(key_noise, (TOKENS, N), jnp.float32)
    return (values * scales).astype(jnp.bfloat16)


def level_of(own_key, extent, cuts, least, largest):
    level = 1.0
    for dim, parts in cuts:
        steps = jax.random.uniform(jax.random.fold_in(jax.random.fold_in(own_key, 6), dim), (parts,), jnp.float32, least / len(cuts), largest / len(cuts))
        level = level * jnp.repeat(jnp.exp(steps), extent[dim] // parts).reshape((-1,) + (1,) * (len(extent) - 1 - dim))
    return level


def setup_inputs(seed: int = 0) -> dict:
    key_of = jax.random.split(jax.random.key(seed), 5)
    return {
        "activations": draw_activations(jax.random.fold_in(key_of[4], 71), 0),
        "cotangents": draw_cotangents(jax.random.fold_in(key_of[4], 71), 0),
        "row_second": jnp.clip(jnp.exp(math.log(0.3) - 4.6051702 * jax.random.uniform(key_of[2], (ROWS,), jnp.float32) ** level_of(key_of[2], (ROWS,), ((0, 64),), -0.2, 0.2)), 0.003, 0.3),
        "column_second": jnp.clip(jnp.exp(math.log(0.3) - 4.6051702 * jax.random.uniform(key_of[3], (N,), jnp.float32) ** level_of(key_of[3], (N,), ((0, 8),), -0.2, 0.2)), 0.003, 0.3),
    }


decay_rate = 1.0 - 10.0 ** (-0.8)

def reference(activations, cotangents, row_second, column_second):
    gradient = lax.dot_general(activations, cotangents, (((0,), (0,)), ((), ())), preferred_element_type=jnp.float32)
    height = gradient.shape[0]
    width = gradient.shape[1]
    entries = height * width
    factor = 1.0 / jnp.maximum(1.0, jnp.sqrt(jnp.sum(gradient * gradient) / entries + 1e-06))
    scaled = gradient * factor
    squares = scaled * scaled
    row_moment = decay_rate * row_second + (1.0 - decay_rate) * lax.optimization_barrier(jnp.sum(squares, axis=1)) / width
    column_moment = decay_rate * column_second + (1.0 - decay_rate) * lax.optimization_barrier(jnp.sum(squares, axis=0)) / height
    row_mean = jnp.sum(row_moment) / height
    unclipped = scaled / jnp.sqrt(row_moment[:, None] * column_moment[None, :] / row_mean)
    update_rms = jnp.sqrt(jnp.sum(unclipped * unclipped) / entries + 1e-06)
    update = unclipped / jnp.maximum(1.0, update_rms)
    return (update, row_moment, column_moment)
```

```python
import jax
import jax.numpy as jnp
from jax import lax
from jax.experimental import pallas as pl
from jax.experimental.pallas import tpu as pltpu
from jax.sharding import PartitionSpec as P

MESH = pl.DeviceIdType.MESH
F32 = jnp.float32
BF16 = jnp.bfloat16

decay_rate = 1.0 - 10.0 ** (-0.8)

RING = 8
NX, NC = 4, 2
NQ = 3
LENGTHS = ((4, 3), (3, 4))


def far_first(j):
    return lax.rem(4 + (1 - 2 * lax.rem(j, 2)) * ((j + 1) // 2), RING)


def kernel(
    act_hbm, cot_hbm, row_second, col_second,
    update, row_out, col_out,
    act, cot, lhs, grad, got, p2_out, p2_in, fin,
    col_msg, col_in, col_mid, col_in2, row_msg, row_in,
    sum_msg, sum_in, sum_mid, sum_in2,
    load_sem, got_sem, send_sem, p2_sem, p2_send, col_sem, row_sem, sum_sem, small_send,
):
    tokens, height = act.shape
    wide = cot.shape[2]
    rows = height // RING
    part = rows // 2
    own = rows // RING
    width = 2 * NQ * wide * NX * NC
    entries = height * width

    dp, mp = lax.axis_index("dp"), lax.axis_index("mp")
    z, y = dp // RING, lax.rem(dp, RING)
    me = (z, y)

    def ring(h, pos):
        pos = lax.rem(pos + RING, RING)
        return (pos * RING + y, mp) if h == 0 else (z * RING + pos, mp)

    load_act = pltpu.make_async_copy(act_hbm, act, load_sem.at[2 * NQ])
    load_act.start()

    def load_cot(k):
        q, h = k // 2, k % 2
        first = (h * NQ + q) * wide
        return pltpu.make_async_copy(
            cot_hbm.at[:, pl.ds(first, wide)], cot.at[h * NQ + q], load_sem.at[h * NQ + q]
        )

    for k in range(2 * NQ):
        load_cot(k).start()

    barrier = pltpu.get_barrier_semaphore()
    for h in (0, 1):
        for d in (1, -1):
            pl.semaphore_signal(barrier, inc=1, device_id=ring(h, me[h] + d), device_id_type=MESH)
    for k in range(1, NX * NC):
        pl.semaphore_signal(
            barrier, inc=1, device_id=(dp, lax.rem(mp + k, NX * NC)), device_id_type=MESH
        )

    p2_out[...] = jnp.zeros_like(p2_out)

    load_act.wait()
    i = lax.broadcasted_iota(jnp.int32, (height, height), 0)
    k = lax.broadcasted_iota(jnp.int32, (height, height), 1)
    blk = i // rows
    rem = i - blk * rows
    sub = rem // own
    swapped = sub * rows + blk * own + (rem - sub * own)
    for h, want in ((0, i), (1, swapped)):
        pick = jnp.where(k == want, 1.0, 0.0).astype(BF16)
        lhs[h] = lax.dot_general(
            pick, act[...], (((1,), (1,)), ((), ())), preferred_element_type=F32
        ).astype(BF16)

    def slot(h, q, p, d, s):
        return ((h * 2 + p) * 7 + (LENGTHS[p][0] if d else 0) + s) * NQ + q

    def hop(h, q, p, d, s):
        way = 1 if d == 0 else -1
        dest = lax.rem(me[h] + way * (LENGTHS[p][d] - s) + RING, RING)
        n = slot(h, q, p, d, s)
        return dest, pltpu.make_async_remote_copy(
            src_ref=grad.at[h, q, dest, p], dst_ref=got.at[n],
            send_sem=send_sem, recv_sem=got_sem.at[n],
            device_id=ring(h, me[h] + way), device_id_type=MESH,
        )

    def landed(h, q, p, d, s):
        n = slot(h, q, p, d, s)
        pltpu.make_async_copy(got.at[n], got.at[n], got_sem.at[n]).wait()
        return got[n]

    for k in range(2 * NQ):
        q, h = k // 2, k % 2
        load_cot(k).wait()
        product = jnp.dot(lhs[h], cot[h * NQ + q], preferred_element_type=F32)
        grad[h, q] = product.reshape(RING, 2, part, wide)
        if k == 0:
            pl.semaphore_wait(barrier, 4 + NX * NC - 1)
        for p in (0, 1):
            for d in (0, 1):
                hop(h, q, p, d, 0)[1].start()

    for s in range(1, 4):

        def step(q, carry, s=s):
            for p in (0, 1):
                for h in (0, 1):
                    for d in (0, 1):
                        if s < LENGTHS[p][d]:
                            block = landed(h, q, p, d, s - 1)
                            dest, copy = hop(h, q, p, d, s)
                            grad[h, q, dest, p] += block
                            copy.start()
            return carry

        lax.fori_loop(0, NQ, step, 0)

    def last(q, carry):
        for p in (0, 1):
            for h in (0, 1):
                block = grad[h, q, me[h], p]
                for d in (0, 1):
                    block += landed(h, q, p, d, LENGTHS[p][d] - 1)
                for j in range(RING // 2):
                    p2_out[h, q, p * (RING // 2) + j, 0:own] = block[j * own : (j + 1) * own]
        for h in (0, 1):
            for j in range(RING):

                @pl.when(j != me[1 - h])
                def _(h=h, j=j):
                    pltpu.make_async_remote_copy(
                        src_ref=p2_out.at[h, q, j], dst_ref=p2_in.at[h, q, me[1 - h]],
                        send_sem=p2_send, recv_sem=p2_sem.at[h * NQ + q],
                        device_id=ring(1 - h, j), device_id_type=MESH,
                    ).start()

            p2_in[h, q, me[1 - h]] = p2_out[h, q, me[1 - h]]
        return carry

    lax.fori_loop(0, NQ, last, 0)

    row_sum = jnp.zeros((8, 1), F32)
    for q in range(NQ):
        for h in (0, 1):
            seven = p2_in.at[h, q, pl.ds(0, RING - 1)]
            pltpu.make_async_copy(seven, seven, p2_sem.at[h * NQ + q]).wait()
            total = p2_in[h, q, 0]
            for j in range(1, RING):
                total += p2_in[h, q, j]
            fin[h * NQ + q] = total
            squares = total * total
            row_sum += jnp.sum(squares, axis=1, keepdims=True)
            col_msg[h * NQ + q] = jnp.sum(squares, axis=0, keepdims=True)

    def ring_all(h, msg, landing, recv):
        def send(j, carry):
            pltpu.make_async_remote_copy(
                src_ref=msg, dst_ref=landing.at[me[h]],
                send_sem=small_send, recv_sem=recv,
                device_id=ring(h, me[h] + far_first(j)), device_id_type=MESH,
            ).start()
            return carry

        lax.fori_loop(0, RING - 1, send, 0)
        landing[me[h]] = msg[...]

    def ring_wait(landing, sem):
        seven = landing.at[pl.ds(0, RING - 1)]
        pltpu.make_async_copy(seven, seven, sem).wait()

    def plane_all(msg, landing, recv):
        def send(j, carry):
            pos = lax.rem(y + far_first(j // (NX * NC)), RING)
            other = lax.rem(mp + NX + lax.rem(j, NX * NC), NX * NC)

            @pl.when(jnp.logical_or(pos != y, other != mp))
            def _():
                pltpu.make_async_remote_copy(
                    src_ref=msg, dst_ref=landing.at[y * (NX * NC) + mp],
                    send_sem=small_send, recv_sem=recv,
                    device_id=(z * RING + pos, other), device_id_type=MESH,
                ).start()

            return carry

        lax.fori_loop(0, RING * NX * NC, send, 0)
        landing[y * (NX * NC) + mp] = msg[...]

    def plane_wait(landing, sem):
        rest = landing.at[pl.ds(0, RING * NX * NC - 1)]
        pltpu.make_async_copy(rest, rest, sem).wait()

    lane = lax.broadcasted_iota(jnp.int32, (1, 128), 1)
    sub8 = lax.broadcasted_iota(jnp.int32, (8, 128), 0)
    second = jnp.full((8, 128), 1.0, F32)
    second_sum = row_second[0]
    for r in range(own):
        second = jnp.where(sub8 == r, row_second[r], second)
        if r:
            second_sum = second_sum + row_second[r]

    part_sum = jnp.sum(row_sum, axis=0, keepdims=True)
    sum_msg[0] = jnp.where(lane < 64, part_sum, second_sum)
    plane_all(sum_msg.at[0], sum_in.at[0], sum_sem.at[0])

    row_msg[...] = jnp.broadcast_to(row_sum, (8, 128))

    def send_rows(k, carry):
        pltpu.make_async_remote_copy(
            src_ref=row_msg, dst_ref=row_in.at[mp],
            send_sem=small_send, recv_sem=row_sem,
            device_id=(dp, lax.rem(mp + k, NX * NC)), device_id_type=MESH,
        ).start()
        return carry

    ring_all(0, col_msg, col_in, col_sem.at[0])
    lax.fori_loop(1, NX * NC, send_rows, 0)
    row_in[mp] = row_msg[...]

    plane_wait(sum_in.at[0], sum_sem.at[0])
    sum_mid[0] = jnp.sum(sum_in[0], axis=0)
    ring_all(0, sum_mid.at[0], sum_in2.at[0], sum_sem.at[1])

    ring_wait(col_in, col_sem.at[0])
    col_mid[...] = jnp.sum(col_in[...], axis=0)
    ring_all(1, col_mid, col_in2, col_sem.at[1])

    rest = row_in.at[pl.ds(0, NX * NC - 1)]
    pltpu.make_async_copy(rest, rest, row_sem).wait()
    row_total = jnp.sum(row_in[...], axis=0)

    ring_wait(sum_in2.at[0], sum_sem.at[1])
    both = jnp.sum(sum_in2[0], axis=0)
    grand = both[:, 0:1]
    second_all = both[:, 64:65] / (NX * NC)
    factor = 1.0 / jnp.maximum(1.0, jnp.sqrt(grand / entries + 1e-06))
    square = factor * factor
    row_moment = decay_rate * second + (1.0 - decay_rate) * (square * row_total) / width
    row_mean = (decay_rate * second_all + (1.0 - decay_rate) * (square * grand) / width) / height
    row_scale = (factor * lax.rsqrt(row_moment / row_mean))[:, 0:1]
    lane8 = lax.broadcasted_iota(jnp.int32, (8, 128), 1)
    row_out[...] = jnp.sum(jnp.where(sub8 == lane8, row_moment, 0.0), axis=0, keepdims=True)

    ring_wait(col_in2, col_sem.at[1])
    rms_sum = jnp.zeros((8, 1), F32)
    for k in range(2 * NQ):
        column = jnp.sum(col_in2[:, k], axis=0)
        moment = (
            decay_rate * col_second[:, k * wide : (k + 1) * wide]
            + (1.0 - decay_rate) * (square * column) / height
        )
        col_out[:, k * wide : (k + 1) * wide] = moment
        unclipped = fin[k] * row_scale * lax.rsqrt(moment)
        fin[k] = unclipped
        rms_sum += jnp.sum(unclipped * unclipped, axis=1, keepdims=True)

    sum_msg[1] = jnp.broadcast_to(jnp.sum(rms_sum, axis=0, keepdims=True), (1, 128))
    plane_all(sum_msg.at[1], sum_in.at[1], sum_sem.at[2])
    plane_wait(sum_in.at[1], sum_sem.at[2])
    sum_mid[1] = jnp.sum(sum_in[1], axis=0)
    ring_all(0, sum_mid.at[1], sum_in2.at[1], sum_sem.at[3])

    pltpu.make_async_copy(got, got, send_sem).wait()
    seven = p2_in.at[:, :, pl.ds(0, RING - 1)]
    pltpu.make_async_copy(seven, seven, p2_send).wait()
    for landing in (col_in, col_in2):
        ring_wait(landing, small_send)
    pltpu.make_async_copy(rest, rest, small_send).wait()
    for n in (0, 1):
        plane_wait(sum_in.at[n], small_send)
        ring_wait(sum_in2.at[n], small_send)

    ring_wait(sum_in2.at[1], sum_sem.at[3])
    square_sum = jnp.sum(sum_in2[1], axis=0)[:, 0:1]
    clip = 1.0 / jnp.maximum(1.0, jnp.sqrt(square_sum / entries + 1e-06))
    for k in range(2 * NQ):
        update[:, k * wide : (k + 1) * wide] = fin[k, 0:own] * clip


def per_device(activations, cotangents, row_second, column_second):
    tokens, height = activations.shape
    columns = cotangents.shape[1]
    own = row_second.shape[0]
    wide = columns // (2 * NQ)
    rows = height // RING
    slots = NX * NC * RING
    vmem = pl.BlockSpec(memory_space=pltpu.VMEM)
    smem = pl.BlockSpec(memory_space=pltpu.SMEM)
    hbm = pl.BlockSpec(memory_space=pl.ANY)
    dma = pltpu.SemaphoreType.DMA
    update, row_moment, column_moment = pl.pallas_call(
        kernel,
        out_shape=(
            jax.ShapeDtypeStruct((own, columns), F32),
            jax.ShapeDtypeStruct((1, 128), F32),
            jax.ShapeDtypeStruct((1, columns), F32),
        ),
        in_specs=[hbm, hbm, smem, vmem],
        out_specs=(vmem, vmem, vmem),
        scratch_shapes=[
            pltpu.VMEM((tokens, height), BF16),
            pltpu.VMEM((2 * NQ, tokens, wide), BF16),
            pltpu.VMEM((2, height, tokens), BF16),
            pltpu.VMEM((2, NQ, RING, 2, rows // 2, wide), F32),
            pltpu.VMEM((2 * NQ * 2 * 7, rows // 2, wide), F32),
            pltpu.VMEM((2, NQ, RING, 8, wide), F32),
            pltpu.VMEM((2, NQ, RING, 8, wide), F32),
            pltpu.VMEM((2 * NQ, 8, wide), F32),
            pltpu.VMEM((2 * NQ, 1, wide), F32),
            pltpu.VMEM((RING, 2 * NQ, 1, wide), F32),
            pltpu.VMEM((2 * NQ, 1, wide), F32),
            pltpu.VMEM((RING, 2 * NQ, 1, wide), F32),
            pltpu.VMEM((8, 128), F32),
            pltpu.VMEM((NX * NC, 8, 128), F32),
            pltpu.VMEM((2, 1, 128), F32),
            pltpu.VMEM((2, slots, 1, 128), F32),
            pltpu.VMEM((2, 1, 128), F32),
            pltpu.VMEM((2, RING, 1, 128), F32),
            dma((2 * NQ + 1,)),
            dma((2 * NQ * 2 * 7,)),
            dma,
            dma((2 * NQ,)),
            dma,
            dma((2,)),
            dma,
            dma((4,)),
            dma,
        ],
        compiler_params=pltpu.CompilerParams(
            collective_id=0, has_side_effects=True, vmem_limit_bytes=48 * 2**20
        ),
    )(activations, cotangents, row_second, column_second.reshape(1, columns))
    return update, row_moment[0, :own], column_moment.reshape(columns)


def solution(mesh):
    placed = (P("dp", None), P("dp", "mp"), P("dp"), P("mp"))
    return jax.shard_map(
        per_device,
        mesh=mesh,
        in_specs=placed,
        out_specs=(P("dp", "mp"), P("dp"), P("mp")),
        check_vma=False,
    )
```

```python
import functools

import jax
import jax.numpy as jnp
from jax import lax
from jax.experimental import pallas as pl
from jax.experimental.pallas import tpu as pltpu
from jax.sharding import PartitionSpec as P

MESH = pl.DeviceIdType.MESH
F32 = jnp.float32
BF16 = jnp.bfloat16

decay_rate = 1.0 - 10.0 ** (-0.8)

RING = 8
NX, NC = 4, 2
MP = NX * NC
SLOTS = RING * MP
WIDTHS = (384, 384, 384)
LENGTHS = ((4, 3), (3, 4))
FAR_FIRST = (4, 3, 5, 2, 6, 1, 7)
FAR_FIRST_X = (2, 1, 3, 0)


def tree_sum(values):
    n = values.shape[0]
    while n > 1:
        n //= 2
        values = values[:n] + values[n : 2 * n]
    return values[0]


def kernel(
    act_hbm, cot_hbm, row_hbm, col_hbm,
    update, row_out, col_out,
    row_second, col_second, act, lhs,
    cot, grad, got, p2_out, p2_in, fin, col_msg, col_in, col_mid, col_in2,
    row_msg, row_in, sum_msg, sum_in, sum_mid, sum_in2,
    load_sem, got_sem, send_sem, p2_sem, p2_send, col_sem, col_send,
    row_sem, row_send, sum_sem, sum_send,
):
    height = act.shape[1]
    rows = height // RING
    part = rows // 2
    own = rows // RING
    half = sum(WIDTHS)
    width = 2 * half * MP
    entries = height * width
    chunks = range(len(WIDTHS))

    dp, mp = lax.axis_index("dp"), lax.axis_index("mp")
    z, y = dp // RING, lax.rem(dp, RING)
    x, core = mp // NC, lax.rem(mp, NC)
    me = (z, y)

    def around(pos):
        return lax.rem(pos + RING, RING)

    def ring(h, pos):
        return (pos * RING + y, mp) if h == 0 else (z * RING + pos, mp)

    def send(src, dst, send, recv, device):
        pltpu.make_async_remote_copy(
            src_ref=src, dst_ref=dst, send_sem=send, recv_sem=recv,
            device_id=device, device_id_type=MESH,
        ).start()

    def wait_for(ref, sem):
        pltpu.make_async_copy(ref, ref, sem).wait()

    barrier = pltpu.get_barrier_semaphore()
    for h in (0, 1):
        for d in (1, -1):
            pl.semaphore_signal(
                barrier, inc=1, device_id=ring(h, around(me[h] + d)), device_id_type=MESH
            )
    for k in range(1, MP):
        pl.semaphore_signal(
            barrier, inc=1, device_id=(dp, lax.rem(mp + k, MP)), device_id_type=MESH
        )

    def first_column(h, q):
        return h * half + sum(WIDTHS[:q])

    def load(src, dst, n):
        return pltpu.make_async_copy(src, dst, load_sem.at[n])

    def load_cot(h, q):
        columns = pl.ds(first_column(h, q), WIDTHS[q])
        return load(cot_hbm.at[:, columns], cot[q].at[h], 3 + 2 * q + h)

    load_act = load(act_hbm, act, 0)
    load_act.start()
    for q in chunks:
        for h in (0, 1):
            load_cot(h, q).start()
    load_row = load(row_hbm, row_second, 1)
    load_col = load(col_hbm, col_second, 2)
    load_row.start()
    load_col.start()

    def transposed(h):
        i = lax.broadcasted_iota(jnp.int32, (height, height), 0)
        k = lax.broadcasted_iota(jnp.int32, (height, height), 1)
        want = i
        if h:
            block = i // rows
            rest = i - block * rows
            sub = rest // own
            want = sub * rows + block * own + (rest - sub * own)
        pick = jnp.where(k == want, 1.0, 0.0).astype(BF16)
        lhs[h] = lax.dot_general(
            pick, act[...], (((1,), (1,)), ((), ())), preferred_element_type=F32
        ).astype(BF16)

    def slot(h, p, d, s):
        return (h * 2 + p) * 7 + (LENGTHS[p][0] if d else 0) + s

    def hop(h, q, p, d, s):
        way = 1 if d == 0 else -1
        dest = around(me[h] + way * (LENGTHS[p][d] - s))
        if s:
            grad[q][h, dest, p] += landed(h, q, p, d, s - 1)
        n = slot(h, p, d, s)
        send(
            grad[q].at[h, dest, p], got[q].at[n], send_sem.at[q], got_sem.at[28 * q + n],
            ring(h, around(me[h] + way)),
        )

    def landed(h, q, p, d, s):
        n = slot(h, p, d, s)
        wait_for(got[q].at[n], got_sem.at[28 * q + n])
        return got[q][n]

    load_act.wait()
    for q in chunks:
        for h in (0, 1):
            if q == 0:
                transposed(h)
            load_cot(h, q).wait()
            product = jnp.dot(lhs[h], cot[q][h], preferred_element_type=F32)
            grad[q][h] = product.reshape(RING, 2, part, WIDTHS[q])
            if q == 0 and h == 0:
                pl.semaphore_wait(barrier, 4 + MP - 1)
            for p in (0, 1):
                for d in (0, 1):
                    hop(h, q, p, d, 0)

    for s in range(1, 4):
        for q in chunks:
            for p in (0, 1):
                for h in (0, 1):
                    for d in (0, 1):
                        if s < LENGTHS[p][d]:
                            hop(h, q, p, d, s)

    for q in chunks:
        for p in (0, 1):
            for h in (0, 1):
                block = grad[q][h, me[h], p]
                for d in (0, 1):
                    block += landed(h, q, p, d, LENGTHS[p][d] - 1)
                for j in range(RING // 2):
                    p2_out[q][h, p * (RING // 2) + j] = block[j * own : (j + 1) * own]
        for offset in FAR_FIRST:
            for h in (0, 1):
                dest = around(me[1 - h] + offset)
                send(
                    p2_out[q].at[h, dest], p2_in[q].at[h, me[1 - h]],
                    p2_send.at[q], p2_sem.at[2 * q + h], ring(1 - h, dest),
                )
        for h in (0, 1):
            p2_in[q][h, me[1 - h]] = p2_out[q][h, me[1 - h]]

    def ring_send(h, msg, landing, sem, recv):
        for offset in FAR_FIRST:
            send(msg, landing.at[me[h]], sem, recv, ring(h, around(me[h] + offset)))
        landing[me[h]] = msg[...]

    def ring_wait(landing, sem):
        wait_for(landing.at[pl.ds(0, RING - 1)], sem)

    def sum_send_all(n):
        mine = y * MP + mp
        for dy in (*FAR_FIRST, 0):
            for dx in FAR_FIRST_X:
                to = (z * RING + around(y + dy), lax.rem(x + dx, NX) * NC + 1)
                go = functools.partial(
                    send, sum_msg.at[n], sum_in.at[n, mine], sum_send.at[n], sum_sem.at[2 * n], to
                )
                if dy or dx:
                    go()
                else:
                    pl.when(core == 0)(go)

    def sum_pass_on(n):
        mine = y * MP + mp

        @pl.when(core == 1)
        def _():
            sum_in[n, mine] = sum_msg[n]
            wait_for(sum_in.at[n, pl.ds(0, SLOTS - 1)], sum_sem.at[2 * n])
            sum_mid[n] = tree_sum(sum_in[n])
            for dz in FAR_FIRST:
                for c in (0, 1):
                    to = (around(z + dz) * RING + y, x * NC + c)
                    send(
                        sum_mid.at[n], sum_in2.at[n, z], sum_send.at[n], sum_sem.at[2 * n + 1], to
                    )
            send(
                sum_mid.at[n], sum_in2.at[n, z], sum_send.at[n], sum_sem.at[2 * n + 1],
                (dp, x * NC),
            )
            sum_in2[n, z] = sum_mid[n]

    def sum_sent(n):
        @pl.when(core == 1)
        def _():
            wait_for(sum_in.at[n, pl.ds(0, 46)], sum_send.at[n])

        @pl.when(core == 0)
        def _():
            wait_for(sum_in.at[n, pl.ds(0, 32)], sum_send.at[n])

    def sum_total(n):
        @pl.when(core == 1)
        def _():
            wait_for(sum_in2.at[n, pl.ds(0, RING - 1)], sum_sem.at[2 * n + 1])

        @pl.when(core == 0)
        def _():
            wait_for(sum_in2.at[n], sum_sem.at[2 * n + 1])

        return tree_sum(sum_in2[n])

    load_row.wait()
    load_col.wait()
    lane = lax.broadcasted_iota(jnp.int32, (1, 128), 1)
    sub8 = lax.broadcasted_iota(jnp.int32, (8, 128), 0)
    lane8 = lax.broadcasted_iota(jnp.int32, (8, 128), 1)
    second = jnp.full((8, 128), 1.0, F32)
    second_sum = row_second[0]
    for r in range(own):
        second = jnp.where(sub8 == r, row_second[r], second)
        if r:
            second_sum = second_sum + row_second[r]

    row_sum = jnp.zeros((own, 1), F32)
    for q in chunks:
        for h in (0, 1):
            wait_for(p2_in[q].at[h, pl.ds(0, RING - 1)], p2_sem.at[2 * q + h])
            total = tree_sum(p2_in[q][h])
            fin[q][h] = total
            squares = total * total
            row_sum += jnp.sum(squares, axis=1, keepdims=True)
            col_msg[q][h] = jnp.sum(squares, axis=0, keepdims=True)
        ring_send(0, col_msg[q], col_in[q], col_send.at[q], col_sem.at[2 * q])

    part_sum = jnp.sum(row_sum, axis=0, keepdims=True)
    sum_msg[0] = jnp.where(lane < 64, part_sum, second_sum)
    sum_send_all(0)
    row_msg[...] = jnp.broadcast_to(row_sum, (own, 128))
    for k in range(1, MP):
        send(row_msg, row_in.at[mp], row_send, row_sem, (dp, lax.rem(mp + k, MP)))
    row_in[mp] = row_msg[...]

    for q in chunks:
        ring_wait(col_in[q], col_sem.at[2 * q])
        col_mid[q][...] = tree_sum(col_in[q][...])
        ring_send(1, col_mid[q], col_in2[q], col_send.at[q], col_sem.at[2 * q + 1])

    sum_pass_on(0)

    for q in chunks:
        wait_for(got[q], send_sem.at[q])
        wait_for(p2_in[q].at[:, pl.ds(0, RING - 1)], p2_send.at[q])
    seven = row_in.at[pl.ds(0, MP - 1)]
    wait_for(seven, row_send)
    wait_for(seven, row_sem)
    row_total = tree_sum(row_in[...])

    both = sum_total(0)
    grand = both[:, 0:1]
    second_all = both[:, 64:65] / MP
    factor = 1.0 / jnp.maximum(1.0, jnp.sqrt(grand / entries + 1e-06))
    square = factor * factor
    row_moment = (
        decay_rate * second[:own] + (1.0 - decay_rate) * (square * row_total) / width
    )
    row_mean = (decay_rate * second_all + (1.0 - decay_rate) * (square * grand) / width) / height
    row_scale = (factor * lax.rsqrt(row_moment / row_mean))[:, 0:1]

    rms_sum = jnp.zeros((own, 1), F32)
    for q in chunks:
        ring_wait(col_in2[q], col_sem.at[2 * q + 1])
        column = tree_sum(col_in2[q][...])
        for h in (0, 1):
            columns = slice(first_column(h, q), first_column(h, q) + WIDTHS[q])
            moment = (
                decay_rate * col_second[columns].reshape(1, WIDTHS[q])
                + (1.0 - decay_rate) * (square * column[h]) / height
            )
            col_out[columns] = moment.reshape(WIDTHS[q])
            unclipped = fin[q][h] * row_scale * lax.rsqrt(moment)
            fin[q][h] = unclipped
            rms_sum += jnp.sum(unclipped * unclipped, axis=1, keepdims=True)

    sum_msg[1] = jnp.broadcast_to(jnp.sum(rms_sum, axis=0, keepdims=True), (1, 128))
    sum_send_all(1)
    row_out[...] = jnp.sum(
        jnp.where(sub8[:own] == lane8[:own], row_moment, 0.0), axis=0
    )[0:own]
    sum_pass_on(1)
    for q in chunks:
        for landing in (col_in[q], col_in2[q]):
            ring_wait(landing, col_send.at[q])
    for n in (0, 1):
        sum_sent(n)

    square_sum = sum_total(1)[:, 0:1]
    clip = 1.0 / jnp.maximum(1.0, jnp.sqrt(square_sum / entries + 1e-06))
    for q in chunks:
        for h in (0, 1):
            first = first_column(h, q)
            update[:, first : first + WIDTHS[q]] = fin[q][h] * clip


def write_out(update, row_moment, column_moment, *rest):
    outs, sems = rest[:3], rest[3]
    copies = [
        pltpu.make_async_copy(src, dst, sems.at[n])
        for n, (src, dst) in enumerate(zip((update, row_moment, column_moment), outs))
    ]
    for copy in copies:
        copy.start()
    for copy in copies:
        copy.wait()


def per_device(activations, cotangents, row_second, column_second):
    tokens, height = activations.shape
    columns = cotangents.shape[1]
    own = row_second.shape[0]
    rows = height // RING
    nq = len(WIDTHS)
    vmem = pl.BlockSpec(memory_space=pltpu.VMEM)
    hbm = pl.BlockSpec(memory_space=pltpu.HBM)
    dma = pltpu.SemaphoreType.DMA

    def per_chunk(*shape, dtype=F32):
        return [pltpu.VMEM((*shape, w), dtype) for w in WIDTHS]

    shapes = ((own, columns), (own,), (columns,))
    results = pl.pallas_call(
        kernel,
        out_shape=tuple(pltpu.VMEM(shape, F32) for shape in shapes),
        in_specs=[hbm] * 4,
        out_specs=(vmem,) * 3,
        scratch_shapes=[
            pltpu.SMEM((own,), F32),
            pltpu.VMEM((columns,), F32),
            pltpu.VMEM((tokens, height), BF16),
            pltpu.VMEM((2, height, tokens), BF16),
            per_chunk(2, tokens, dtype=BF16),
            per_chunk(2, RING, 2, rows // 2),
            per_chunk(2 * 2 * 7, rows // 2),
            per_chunk(2, RING, own),
            per_chunk(2, RING, own),
            per_chunk(2, own),
            per_chunk(2, 1),
            per_chunk(RING, 2, 1),
            per_chunk(2, 1),
            per_chunk(RING, 2, 1),
            pltpu.VMEM((own, 128), F32),
            pltpu.VMEM((MP, own, 128), F32),
            pltpu.VMEM((2, 1, 128), F32),
            pltpu.VMEM((2, SLOTS, 1, 128), F32),
            pltpu.VMEM((2, 1, 128), F32),
            pltpu.VMEM((2, RING, 1, 128), F32),
            dma((3 + 2 * nq,)),
            dma((28 * nq,)),
            dma((nq,)),
            dma((2 * nq,)),
            dma((nq,)),
            dma((2 * nq,)),
            dma((nq,)),
            dma,
            dma,
            dma((4,)),
            dma((2,)),
        ],
        compiler_params=pltpu.CompilerParams(
            collective_id=0, has_side_effects=True, vmem_limit_bytes=60 * 2**20
        ),
    )(activations, cotangents, row_second, column_second)
    return pl.pallas_call(
        write_out,
        out_shape=tuple(jax.ShapeDtypeStruct(shape, F32) for shape in shapes),
        in_specs=[vmem] * 3,
        out_specs=(hbm,) * 3,
        scratch_shapes=[dma((3,))],
    )(*[pltpu.with_memory_space_constraint(r, pltpu.VMEM) for r in results])


def solution(mesh):
    placed = (P("dp", None), P("dp", "mp"), P("dp"), P("mp"))
    return jax.shard_map(
        per_device,
        mesh=mesh,
        in_specs=placed,
        out_specs=(P("dp", "mp"), P("dp"), P("mp")),
        check_vma=False,
    )
```

```python
import functools

import jax
import jax.numpy as jnp
from jax import lax
from jax.experimental import pallas as pl
from jax.experimental.pallas import tpu as pltpu
from jax.sharding import PartitionSpec as P

MESH = pl.DeviceIdType.MESH
F32 = jnp.float32
BF16 = jnp.bfloat16

decay_rate = 1.0 - 10.0 ** (-0.8)

RING = 8
NX, NC = 4, 2
MP = NX * NC
SLOTS = RING * MP
WIDTHS = (384, 384, 384)
LENGTHS = ((4, 3), (3, 4))
CHAINS = ((0, 0), (1, 1), (0, 1), (1, 0))
FAR_FIRST = (4, 3, 5, 2, 6, 1, 7)
FAR_FIRST_X = (2, 1, 3, 0)


def tree_sum(values):
    n = values.shape[0]
    while n > 1:
        n //= 2
        values = values[:n] + values[n : 2 * n]
    return values[0]


def lanes(values):
    return sum(values[:, n : n + 128] for n in range(0, values.shape[1], 128))


def kernel(
    act_hbm, cot_hbm, row_hbm, col_hbm,
    update, row_out, col_out,
    row_second, col_second, act, pick, lhs,
    cot, grad, got, p2_out, p2_in, fin, col_msg, col_in, col_mid, col_in2,
    row_msg, row_in, sum_msg, sum_in, sum_mid, sum_in2,
    load_sem, got_sem, send_sem, p2_sem, p2_send, col_sem, col_send,
    row_sem, row_send, sum_sem, sum_send,
):
    height = act.shape[1]
    rows = height // RING
    part = rows // 2
    own = rows // RING
    half = sum(WIDTHS)
    width = 2 * half * MP
    entries = height * width
    chunks = range(len(WIDTHS))

    dp, mp = lax.axis_index("dp"), lax.axis_index("mp")
    z, y = dp // RING, lax.rem(dp, RING)
    x, core = mp // NC, lax.rem(mp, NC)
    me = (z, y)

    def around(pos):
        return lax.rem(pos + RING, RING)

    def ring(h, pos):
        return (pos * RING + y, mp) if h == 0 else (z * RING + pos, mp)

    def send(src, dst, send, recv, device):
        pltpu.make_async_remote_copy(
            src_ref=src, dst_ref=dst, send_sem=send, recv_sem=recv,
            device_id=device, device_id_type=MESH,
        ).start()

    def wait_for(ref, sem):
        pltpu.make_async_copy(ref, ref, sem).wait()

    def first_column(h, q):
        return h * half + sum(WIDTHS[:q])

    def load(src, dst, n):
        return pltpu.make_async_copy(src, dst, load_sem.at[n])

    def load_cot(h, q):
        columns = pl.ds(first_column(h, q), WIDTHS[q])
        return load(cot_hbm.at[:, columns], cot[q].at[h], 3 + 2 * q + h)

    load_act = load(act_hbm, act, 0)
    load_act.start()
    for h in (0, 1):
        load_cot(h, 0).start()

    barrier = pltpu.get_barrier_semaphore()
    for h in (0, 1):
        for d in (1, -1):
            pl.semaphore_signal(
                barrier, inc=1, device_id=ring(h, around(me[h] + d)), device_id_type=MESH
            )
    for k in range(1, MP):
        pl.semaphore_signal(
            barrier, inc=1, device_id=(dp, lax.rem(mp + k, MP)), device_id_type=MESH
        )

    for q in chunks[1:]:
        for h in (0, 1):
            load_cot(h, q).start()
    load_row = load(row_hbm, row_second, 1)
    load_col = load(col_hbm, col_second, 2)
    load_row.start()
    load_col.start()

    i = lax.broadcasted_iota(jnp.int32, (height, height), 0)
    k = lax.broadcasted_iota(jnp.int32, (height, height), 1)
    block = i // rows
    sub = (i - block * rows) // own
    want = i + (sub - block) * (rows - own)
    pick[...] = jnp.where(k == want, 1.0, 0.0).astype(BF16)

    def slot(h, p, d, s):
        return (h * 2 + p) * 7 + (LENGTHS[p][0] if d else 0) + s

    def hop(h, q, p, d, s):
        way = 1 if d == 0 else -1
        dest = around(me[h] + way * (LENGTHS[p][d] - s))
        if s:
            grad[q][h, dest, p] += landed(h, q, p, d, s - 1)
        n = slot(h, p, d, s)
        send(
            grad[q].at[h, dest, p], got[q].at[n], send_sem.at[q], got_sem.at[28 * q + n],
            ring(h, around(me[h] + way)),
        )

    def landed(h, q, p, d, s):
        n = slot(h, p, d, s)
        wait_for(got[q].at[n], got_sem.at[28 * q + n])
        return got[q][n]

    load_act.wait()
    for q in chunks:
        for h in (0, 1):
            if q == 0 and h == 1:
                lhs[...] = lax.dot_general(
                    pick[...], act[...], (((1,), (1,)), ((), ())), preferred_element_type=F32
                ).astype(BF16)
            load_cot(h, q).wait()
            if h == 0:
                product = lax.dot_general(
                    act[...], cot[q][h], (((0,), (0,)), ((), ())), preferred_element_type=F32
                )
            else:
                product = jnp.dot(lhs[...], cot[q][h], preferred_element_type=F32)
            grad[q][h] = product.reshape(RING, 2, part, WIDTHS[q])
            if q == 0 and h == 0:
                pl.semaphore_wait(barrier, 4 + MP - 1)
            for p, d in CHAINS:
                hop(h, q, p, d, 0)

    for s in range(1, 4):
        for q in chunks:
            for p, d in CHAINS:
                for h in (0, 1):
                    if s < LENGTHS[p][d]:
                        hop(h, q, p, d, s)
                    else:
                        grad[q][h, me[h], p] += landed(h, q, p, d, s - 1)

    for q in chunks:
        for h in (0, 1):
            for p in (0, 1):
                block = grad[q][h, me[h], p] + landed(h, q, p, p, 3)
                for j in range(RING // 2):
                    dest = p * (RING // 2) + j
                    p2_out[q][h, dest] = block[j * own : (j + 1) * own]
            for offset in FAR_FIRST:
                dest = around(me[1 - h] + offset)
                send(
                    p2_out[q].at[h, dest], p2_in[q].at[h, me[1 - h]],
                    p2_send.at[q], p2_sem.at[2 * q + h], ring(1 - h, dest),
                )
        for h in (0, 1):
            p2_in[q][h, me[1 - h]] = p2_out[q][h, me[1 - h]]

    def ring_send(h, msg, landing, sem, recv):
        for offset in FAR_FIRST:
            send(msg, landing.at[me[h]], sem, recv, ring(h, around(me[h] + offset)))
        landing[me[h]] = msg[...]

    def ring_wait(landing, sem):
        wait_for(landing.at[pl.ds(0, RING - 1)], sem)

    def sum_send_all(n):
        mine = y * MP + mp
        for dy in (*FAR_FIRST, 0):
            for dx in FAR_FIRST_X:
                to = (z * RING + around(y + dy), lax.rem(x + dx, NX) * NC + 1)
                go = functools.partial(
                    send, sum_msg.at[n], sum_in.at[n, mine], sum_send.at[n], sum_sem.at[2 * n], to
                )
                if dy or dx:
                    go()
                else:
                    pl.when(core == 0)(go)

    def sum_pass_on(n):
        mine = y * MP + mp

        @pl.when(core == 1)
        def _():
            sum_in[n, mine] = sum_msg[n]
            wait_for(sum_in.at[n, pl.ds(0, SLOTS - 1)], sum_sem.at[2 * n])
            sum_mid[n] = tree_sum(sum_in[n])
            for dz in FAR_FIRST:
                for c in (0, 1):
                    to = (around(z + dz) * RING + y, x * NC + c)
                    send(
                        sum_mid.at[n], sum_in2.at[n, z], sum_send.at[n], sum_sem.at[2 * n + 1], to
                    )
            send(
                sum_mid.at[n], sum_in2.at[n, z], sum_send.at[n], sum_sem.at[2 * n + 1],
                (dp, x * NC),
            )
            sum_in2[n, z] = sum_mid[n]

    def sum_sent(n):
        @pl.when(core == 1)
        def _():
            wait_for(sum_in.at[n, pl.ds(0, 46)], sum_send.at[n])

        @pl.when(core == 0)
        def _():
            wait_for(sum_in.at[n, pl.ds(0, 32)], sum_send.at[n])

    def sum_total(n):
        @pl.when(core == 1)
        def _():
            wait_for(sum_in2.at[n, pl.ds(0, RING - 1)], sum_sem.at[2 * n + 1])

        @pl.when(core == 0)
        def _():
            wait_for(sum_in2.at[n], sum_sem.at[2 * n + 1])

        return tree_sum(sum_in2[n])

    load_row.wait()
    load_col.wait()
    sub8 = lax.broadcasted_iota(jnp.int32, (8, 128), 0)
    lane8 = lax.broadcasted_iota(jnp.int32, (8, 128), 1)
    second = jnp.full((8, 128), 1.0, F32)
    second_sum = row_second[0]
    for r in range(own):
        second = jnp.where(sub8 == r, row_second[r], second)
        if r:
            second_sum = second_sum + row_second[r]

    sum_msg[0, 1:2] = jnp.full((1, 128), second_sum, F32)
    sum_msg[1] = jnp.zeros((2, 128), F32)
    row_sum = jnp.zeros((own, 128), F32)
    for q in chunks:
        for h in (0, 1):
            wait_for(p2_in[q].at[h, pl.ds(0, RING - 1)], p2_sem.at[2 * q + h])
            total = tree_sum(p2_in[q][h])
            fin[q][h] = total
            squares = total * total
            row_sum += lanes(squares)
            col_msg[q][h] = jnp.sum(squares, axis=0, keepdims=True)
        ring_send(0, col_msg[q], col_in[q], col_send.at[q], col_sem.at[2 * q])

    sum_msg[0, 0:1] = jnp.sum(row_sum, axis=0, keepdims=True)
    sum_send_all(0)
    row_msg[...] = row_sum
    for k in range(1, MP):
        send(row_msg, row_in.at[mp], row_send, row_sem, (dp, lax.rem(mp + k, MP)))
    row_in[mp] = row_msg[...]

    for q in chunks:
        ring_wait(col_in[q], col_sem.at[2 * q])
        col_mid[q][...] = tree_sum(col_in[q][...])
        ring_send(1, col_mid[q], col_in2[q], col_send.at[q], col_sem.at[2 * q + 1])

    sum_pass_on(0)

    for q in chunks:
        wait_for(got[q], send_sem.at[q])
        wait_for(p2_in[q].at[:, pl.ds(0, RING - 1)], p2_send.at[q])
    seven = row_in.at[pl.ds(0, MP - 1)]
    wait_for(seven, row_send)
    wait_for(seven, row_sem)
    row_total = jnp.sum(tree_sum(row_in[...]), axis=1, keepdims=True)

    column_sums = []
    for q in chunks:
        ring_wait(col_in2[q], col_sem.at[2 * q + 1])
        column_sums.append(tree_sum(col_in2[q][...]))

    both = sum_total(0)
    grand = jnp.sum(both[0:1], axis=1, keepdims=True)
    second_all = both[1:2, 0:1] / MP
    factor = 1.0 / jnp.maximum(1.0, jnp.sqrt(grand / entries + 1e-06))
    square = factor * factor
    row_moment = (
        decay_rate * second[:own, 0:1] + (1.0 - decay_rate) * (square * row_total) / width
    )
    row_mean = (decay_rate * second_all + (1.0 - decay_rate) * (square * grand) / width) / height
    row_scale = factor * lax.rsqrt(row_moment / row_mean)

    rms_sum = jnp.zeros((own, 128), F32)
    for q in chunks:
        for h in (0, 1):
            columns = slice(first_column(h, q), first_column(h, q) + WIDTHS[q])
            moment = (
                decay_rate * col_second[columns].reshape(1, WIDTHS[q])
                + (1.0 - decay_rate) * (square * column_sums[q][h]) / height
            )
            col_out[columns] = moment.reshape(WIDTHS[q])
            unclipped = fin[q][h] * row_scale * lax.rsqrt(moment)
            fin[q][h] = unclipped
            rms_sum += lanes(unclipped * unclipped)

    sum_msg[1, 0:1] = jnp.sum(rms_sum, axis=0, keepdims=True)
    sum_send_all(1)
    row_out[...] = jnp.sum(
        jnp.where(sub8[:own] == lane8[:own], row_moment, 0.0), axis=0
    )[0:own]
    sum_pass_on(1)
    for q in chunks:
        for landing in (col_in[q], col_in2[q]):
            ring_wait(landing, col_send.at[q])
    for n in (0, 1):
        sum_sent(n)

    square_sum = jnp.sum(sum_total(1)[0:1], axis=1, keepdims=True)
    clip = 1.0 / jnp.maximum(1.0, jnp.sqrt(square_sum / entries + 1e-06))
    for q in chunks:
        for h in (0, 1):
            first = first_column(h, q)
            update[:, first : first + WIDTHS[q]] = fin[q][h] * clip


def write_out(update, row_moment, column_moment, *rest):
    outs, sems = rest[:3], rest[3]
    copies = [
        pltpu.make_async_copy(src, dst, sems.at[n])
        for n, (src, dst) in enumerate(zip((update, row_moment, column_moment), outs))
    ]
    for copy in copies:
        copy.start()
    for copy in copies:
        copy.wait()


def per_device(activations, cotangents, row_second, column_second):
    tokens, height = activations.shape
    columns = cotangents.shape[1]
    own = row_second.shape[0]
    rows = height // RING
    nq = len(WIDTHS)
    vmem = pl.BlockSpec(memory_space=pltpu.VMEM)
    hbm = pl.BlockSpec(memory_space=pltpu.HBM)
    dma = pltpu.SemaphoreType.DMA

    def per_chunk(*shape, dtype=F32):
        return [pltpu.VMEM((*shape, w), dtype) for w in WIDTHS]

    shapes = ((own, columns), (own,), (columns,))
    results = pl.pallas_call(
        kernel,
        out_shape=tuple(pltpu.VMEM(shape, F32) for shape in shapes),
        in_specs=[hbm] * 4,
        out_specs=(vmem,) * 3,
        scratch_shapes=[
            pltpu.SMEM((own,), F32),
            pltpu.VMEM((columns,), F32),
            pltpu.VMEM((tokens, height), BF16),
            pltpu.VMEM((height, height), BF16),
            pltpu.VMEM((height, tokens), BF16),
            per_chunk(2, tokens, dtype=BF16),
            per_chunk(2, RING, 2, rows // 2),
            per_chunk(2 * 2 * 7, rows // 2),
            per_chunk(2, RING, own),
            per_chunk(2, RING, own),
            per_chunk(2, own),
            per_chunk(2, 1),
            per_chunk(RING, 2, 1),
            per_chunk(2, 1),
            per_chunk(RING, 2, 1),
            pltpu.VMEM((own, 128), F32),
            pltpu.VMEM((MP, own, 128), F32),
            pltpu.VMEM((2, 2, 128), F32),
            pltpu.VMEM((2, SLOTS, 2, 128), F32),
            pltpu.VMEM((2, 2, 128), F32),
            pltpu.VMEM((2, RING, 2, 128), F32),
            dma((3 + 2 * nq,)),
            dma((28 * nq,)),
            dma((nq,)),
            dma((2 * nq,)),
            dma((nq,)),
            dma((2 * nq,)),
            dma((nq,)),
            dma,
            dma,
            dma((4,)),
            dma((2,)),
        ],
        compiler_params=pltpu.CompilerParams(
            collective_id=0, has_side_effects=True, vmem_limit_bytes=60 * 2**20
        ),
    )(activations, cotangents, row_second, column_second)
    return pl.pallas_call(
        write_out,
        out_shape=tuple(jax.ShapeDtypeStruct(shape, F32) for shape in shapes),
        in_specs=[vmem] * 3,
        out_specs=(hbm,) * 3,
        scratch_shapes=[dma((3,))],
    )(*[pltpu.with_memory_space_constraint(r, pltpu.VMEM) for r in results])


def solution(mesh):
    placed = (P("dp", None), P("dp", "mp"), P("dp"), P("mp"))
    return jax.shard_map(
        per_device,
        mesh=mesh,
        in_specs=placed,
        out_specs=(P("dp", "mp"), P("dp"), P("mp")),
        check_vma=False,
    )
```

```python
import functools

import jax
import jax.numpy as jnp
from jax import lax
from jax.experimental import pallas as pl
from jax.experimental.pallas import tpu as pltpu
from jax.sharding import PartitionSpec as P

MESH = pl.DeviceIdType.MESH
F32 = jnp.float32
BF16 = jnp.bfloat16

decay_rate = 1.0 - 10.0 ** (-0.8)

RING = 8
NX, NC = 4, 2
MP = NX * NC
SLOTS = RING * MP
WIDTHS = (384, 384, 384)
LENGTHS = ((4, 3), (3, 4))
CHAINS = ((0, 0), (1, 1), (0, 1), (1, 0))
FAR_FIRST = (4, 3, 5, 2, 6, 1, 7)
FAR_FIRST_X = (2, 1, 3, 0)


def tree_sum(values):
    n = values.shape[0]
    while n > 1:
        n //= 2
        values = values[:n] + values[n : 2 * n]
    return values[0]


def lanes(values):
    return sum(values[:, n : n + 128] for n in range(0, values.shape[1], 128))


def kernel(
    act_hbm, cot_hbm, row_hbm, col_hbm,
    update, row_out, col_out,
    row_second, col_second, act, pick, lhs,
    cot, grad, got, p2_out, p2_in, fin, col_msg, col_in, col_mid, col_in2,
    row_msg, row_in, sum_msg, sum_in, sum_mid, sum_in2,
    load_sem, got_sem, send_sem, p2_sem, p2_send, col_sem, col_send,
    row_sem, row_send, sum_sem, sum_send,
):
    height = act.shape[1]
    rows = height // RING
    part = rows // 2
    own = rows // RING
    half = sum(WIDTHS)
    width = 2 * half * MP
    entries = height * width
    chunks = range(len(WIDTHS))

    dp, mp = lax.axis_index("dp"), lax.axis_index("mp")
    z, y = dp // RING, lax.rem(dp, RING)
    x, core = mp // NC, lax.rem(mp, NC)
    me = (z, y)

    def around(pos):
        return lax.rem(pos + RING, RING)

    def ring(h, pos):
        return (pos * RING + y, mp) if h == 0 else (z * RING + pos, mp)

    def send(src, dst, send, recv, device):
        pltpu.make_async_remote_copy(
            src_ref=src, dst_ref=dst, send_sem=send, recv_sem=recv,
            device_id=device, device_id_type=MESH,
        ).start()

    def wait_for(ref, sem):
        pltpu.make_async_copy(ref, ref, sem).wait()

    def first_column(h, q):
        return h * half + sum(WIDTHS[:q])

    def load(src, dst, n):
        return pltpu.make_async_copy(src, dst, load_sem.at[n])

    def load_cot(h, q):
        columns = pl.ds(first_column(h, q), WIDTHS[q])
        return load(cot_hbm.at[:, columns], cot[q].at[h], 3 + 2 * q + h)

    load_act = load(act_hbm, act, 0)
    load_act.start()
    for h in (0, 1):
        load_cot(h, 0).start()

    barrier = pltpu.get_barrier_semaphore()
    for h in (0, 1):
        for d in (1, -1):
            pl.semaphore_signal(
                barrier, inc=1, device_id=ring(h, around(me[h] + d)), device_id_type=MESH
            )
    for k in range(1, MP):
        pl.semaphore_signal(
            barrier, inc=1, device_id=(dp, lax.rem(mp + k, MP)), device_id_type=MESH
        )

    for q in chunks[1:]:
        for h in (0, 1):
            load_cot(h, q).start()
    load_row = load(row_hbm, row_second, 1)
    load_col = load(col_hbm, col_second, 2)
    load_row.start()
    load_col.start()

    i = lax.broadcasted_iota(jnp.int32, (height, height), 0)
    k = lax.broadcasted_iota(jnp.int32, (height, height), 1)
    block = i // rows
    sub = (i - block * rows) // own
    want = i + (sub - block) * (rows - own)
    pick[...] = jnp.where(k == want, 1.0, 0.0).astype(BF16)

    def slot(h, p, d, s):
        return (h * 2 + p) * 7 + (LENGTHS[p][0] if d else 0) + s

    def hop(h, q, p, d, s):
        way = 1 if d == 0 else -1
        dest = around(me[h] + way * (LENGTHS[p][d] - s))
        if s:
            grad[q][h, dest, p] += landed(h, q, p, d, s - 1)
        n = slot(h, p, d, s)
        send(
            grad[q].at[h, dest, p], got[q].at[n], send_sem.at[q], got_sem.at[28 * q + n],
            ring(h, around(me[h] + way)),
        )

    def landed(h, q, p, d, s):
        n = slot(h, p, d, s)
        wait_for(got[q].at[n], got_sem.at[28 * q + n])
        return got[q][n]

    load_act.wait()
    for q in chunks:
        for h in (0, 1):
            if q == 0 and h == 1:
                lhs[...] = lax.dot_general(
                    pick[...], act[...], (((1,), (1,)), ((), ())), preferred_element_type=F32
                ).astype(BF16)
            load_cot(h, q).wait()
            if h == 0:
                product = lax.dot_general(
                    act[...], cot[q][h], (((0,), (0,)), ((), ())), preferred_element_type=F32
                )
            else:
                product = jnp.dot(lhs[...], cot[q][h], preferred_element_type=F32)
            grad[q][h] = product.reshape(RING, 2, part, WIDTHS[q])
            if q == 0 and h == 0:
                pl.semaphore_wait(barrier, 4 + MP - 1)
            for p, d in CHAINS:
                hop(h, q, p, d, 0)

    for s in range(1, 4):
        for q in chunks:
            for p, d in CHAINS:
                for h in (0, 1):
                    if s < LENGTHS[p][d]:
                        hop(h, q, p, d, s)
                    else:
                        grad[q][h, me[h], p] += landed(h, q, p, d, s - 1)

    for q in chunks:
        for h in (0, 1):
            for p in (0, 1):
                block = grad[q][h, me[h], p] + landed(h, q, p, p, 3)
                for j in range(RING // 2):
                    dest = p * (RING // 2) + j
                    p2_out[q][h, dest] = block[j * own : (j + 1) * own]
            for offset in FAR_FIRST:
                dest = around(me[1 - h] + offset)
                send(
                    p2_out[q].at[h, dest], p2_in[q].at[h, me[1 - h]],
                    p2_send.at[q], p2_sem.at[2 * q + h], ring(1 - h, dest),
                )
        for h in (0, 1):
            p2_in[q][h, me[1 - h]] = p2_out[q][h, me[1 - h]]

    def ring_send(h, msg, landing, sem, recv):
        for offset in FAR_FIRST:
            send(msg, landing.at[me[h]], sem, recv, ring(h, around(me[h] + offset)))
        landing[me[h]] = msg[...]

    def ring_wait(landing, sem):
        wait_for(landing.at[pl.ds(0, RING - 1)], sem)

    def sum_send_all(n):
        mine = y * MP + mp
        for dy in (*FAR_FIRST, 0):
            for dx in FAR_FIRST_X:
                to = (z * RING + around(y + dy), lax.rem(x + dx, NX) * NC + 1)
                go = functools.partial(
                    send, sum_msg.at[n], sum_in.at[n, mine], sum_send.at[n], sum_sem.at[2 * n], to
                )
                if dy or dx:
                    go()
                else:
                    pl.when(core == 0)(go)

    def sum_pass_on(n):
        mine = y * MP + mp

        @pl.when(core == 1)
        def _():
            sum_in[n, mine] = sum_msg[n]
            wait_for(sum_in.at[n, pl.ds(0, SLOTS - 1)], sum_sem.at[2 * n])
            sum_mid[n] = tree_sum(sum_in[n])
            for dz in FAR_FIRST:
                for c in (0, 1):
                    to = (around(z + dz) * RING + y, x * NC + c)
                    send(
                        sum_mid.at[n], sum_in2.at[n, z], sum_send.at[n], sum_sem.at[2 * n + 1], to
                    )
            send(
                sum_mid.at[n], sum_in2.at[n, z], sum_send.at[n], sum_sem.at[2 * n + 1],
                (dp, x * NC),
            )
            sum_in2[n, z] = sum_mid[n]

    def sum_sent(n):
        @pl.when(core == 1)
        def _():
            wait_for(sum_in.at[n, pl.ds(0, 46)], sum_send.at[n])

        @pl.when(core == 0)
        def _():
            wait_for(sum_in.at[n, pl.ds(0, 32)], sum_send.at[n])

    def sum_total(n):
        @pl.when(core == 1)
        def _():
            wait_for(sum_in2.at[n, pl.ds(0, RING - 1)], sum_sem.at[2 * n + 1])

        @pl.when(core == 0)
        def _():
            wait_for(sum_in2.at[n], sum_sem.at[2 * n + 1])

        return tree_sum(sum_in2[n])

    load_row.wait()
    load_col.wait()
    sub8 = lax.broadcasted_iota(jnp.int32, (8, 128), 0)
    lane8 = lax.broadcasted_iota(jnp.int32, (8, 128), 1)
    second = jnp.full((8, 128), 1.0, F32)
    second_sum = row_second[0]
    for r in range(own):
        second = jnp.where(sub8 == r, row_second[r], second)
        if r:
            second_sum = second_sum + row_second[r]

    sum_msg[0, 1:2] = jnp.full((1, 128), second_sum, F32)
    sum_msg[1] = jnp.zeros((2, 128), F32)
    row_sum = jnp.zeros((own, 128), F32)
    for q in chunks:
        for h in (0, 1):
            wait_for(p2_in[q].at[h, pl.ds(0, RING - 1)], p2_sem.at[2 * q + h])
            total = tree_sum(p2_in[q][h])
            fin[q][h] = total
            squares = total * total
            row_sum += lanes(squares)
            col_msg[q][h] = jnp.sum(squares, axis=0, keepdims=True)
        ring_send(1, col_msg[q], col_in[q], col_send.at[q], col_sem.at[2 * q])

    sum_msg[0, 0:1] = jnp.sum(row_sum, axis=0, keepdims=True)
    sum_send_all(0)
    row_msg[...] = row_sum
    for k in range(1, MP):
        send(row_msg, row_in.at[mp], row_send, row_sem, (dp, lax.rem(mp + k, MP)))
    row_in[mp] = row_msg[...]

    for q in chunks:
        ring_wait(col_in[q], col_sem.at[2 * q])
        col_mid[q][...] = tree_sum(col_in[q][...])
        ring_send(0, col_mid[q], col_in2[q], col_send.at[q], col_sem.at[2 * q + 1])

    sum_pass_on(0)

    for q in chunks:
        wait_for(got[q], send_sem.at[q])
        wait_for(p2_in[q].at[:, pl.ds(0, RING - 1)], p2_send.at[q])
    seven = row_in.at[pl.ds(0, MP - 1)]
    wait_for(seven, row_send)
    wait_for(seven, row_sem)
    row_total = jnp.sum(tree_sum(row_in[...]), axis=1, keepdims=True)

    column_sums = []
    for q in chunks:
        ring_wait(col_in2[q], col_sem.at[2 * q + 1])
        column_sums.append(tree_sum(col_in2[q][...]))

    both = sum_total(0)
    grand = jnp.sum(both[0:1], axis=1, keepdims=True)
    second_all = both[1:2, 0:1] / MP
    factor = 1.0 / jnp.maximum(1.0, jnp.sqrt(grand / entries + 1e-06))
    square = factor * factor
    row_moment = (
        decay_rate * second[:own, 0:1] + (1.0 - decay_rate) * (square * row_total) / width
    )
    row_mean = (decay_rate * second_all + (1.0 - decay_rate) * (square * grand) / width) / height
    row_scale = factor * lax.rsqrt(row_moment / row_mean)

    rms_sum = jnp.zeros((own, 128), F32)
    for q in chunks:
        for h in (0, 1):
            columns = slice(first_column(h, q), first_column(h, q) + WIDTHS[q])
            moment = (
                decay_rate * col_second[columns].reshape(1, WIDTHS[q])
                + (1.0 - decay_rate) * (square * column_sums[q][h]) / height
            )
            col_out[columns] = moment.reshape(WIDTHS[q])
            unclipped = fin[q][h] * row_scale * lax.rsqrt(moment)
            fin[q][h] = unclipped
            rms_sum += lanes(unclipped * unclipped)

    sum_msg[1, 0:1] = jnp.sum(rms_sum, axis=0, keepdims=True)
    sum_send_all(1)
    row_out[...] = jnp.sum(
        jnp.where(sub8[:own] == lane8[:own], row_moment, 0.0), axis=0
    )[0:own]
    sum_pass_on(1)
    for q in chunks:
        for landing in (col_in[q], col_in2[q]):
            ring_wait(landing, col_send.at[q])
    for n in (0, 1):
        sum_sent(n)

    square_sum = jnp.sum(sum_total(1)[0:1], axis=1, keepdims=True)
    clip = 1.0 / jnp.maximum(1.0, jnp.sqrt(square_sum / entries + 1e-06))
    for q in chunks:
        for h in (0, 1):
            first = first_column(h, q)
            update[:, first : first + WIDTHS[q]] = fin[q][h] * clip


def write_out(update, row_moment, column_moment, *rest):
    outs, sems = rest[:3], rest[3]
    copies = [
        pltpu.make_async_copy(src, dst, sems.at[n])
        for n, (src, dst) in enumerate(zip((update, row_moment, column_moment), outs))
    ]
    for copy in copies:
        copy.start()
    for copy in copies:
        copy.wait()


def per_device(activations, cotangents, row_second, column_second):
    tokens, height = activations.shape
    columns = cotangents.shape[1]
    own = row_second.shape[0]
    rows = height // RING
    nq = len(WIDTHS)
    vmem = pl.BlockSpec(memory_space=pltpu.VMEM)
    hbm = pl.BlockSpec(memory_space=pltpu.HBM)
    dma = pltpu.SemaphoreType.DMA

    def per_chunk(*shape, dtype=F32):
        return [pltpu.VMEM((*shape, w), dtype) for w in WIDTHS]

    shapes = ((own, columns), (own,), (columns,))
    results = pl.pallas_call(
        kernel,
        out_shape=tuple(pltpu.VMEM(shape, F32) for shape in shapes),
        in_specs=[hbm] * 4,
        out_specs=(vmem,) * 3,
        scratch_shapes=[
            pltpu.SMEM((own,), F32),
            pltpu.VMEM((columns,), F32),
            pltpu.VMEM((tokens, height), BF16),
            pltpu.VMEM((height, height), BF16),
            pltpu.VMEM((height, tokens), BF16),
            per_chunk(2, tokens, dtype=BF16),
            per_chunk(2, RING, 2, rows // 2),
            per_chunk(2 * 2 * 7, rows // 2),
            per_chunk(2, RING, own),
            per_chunk(2, RING, own),
            per_chunk(2, own),
            per_chunk(2, 1),
            per_chunk(RING, 2, 1),
            per_chunk(2, 1),
            per_chunk(RING, 2, 1),
            pltpu.VMEM((own, 128), F32),
            pltpu.VMEM((MP, own, 128), F32),
            pltpu.VMEM((2, 2, 128), F32),
            pltpu.VMEM((2, SLOTS, 2, 128), F32),
            pltpu.VMEM((2, 2, 128), F32),
            pltpu.VMEM((2, RING, 2, 128), F32),
            dma((3 + 2 * nq,)),
            dma((28 * nq,)),
            dma((nq,)),
            dma((2 * nq,)),
            dma((nq,)),
            dma((2 * nq,)),
            dma((nq,)),
            dma,
            dma,
            dma((4,)),
            dma((2,)),
        ],
        compiler_params=pltpu.CompilerParams(
            collective_id=0, has_side_effects=True, vmem_limit_bytes=60 * 2**20
        ),
    )(activations, cotangents, row_second, column_second)
    return pl.pallas_call(
        write_out,
        out_shape=tuple(jax.ShapeDtypeStruct(shape, F32) for shape in shapes),
        in_specs=[vmem] * 3,
        out_specs=(hbm,) * 3,
        scratch_shapes=[dma((3,))],
    )(*[pltpu.with_memory_space_constraint(r, pltpu.VMEM) for r in results])


def solution(mesh):
    placed = (P("dp", None), P("dp", "mp"), P("dp"), P("mp"))
    return jax.shard_map(
        per_device,
        mesh=mesh,
        in_specs=placed,
        out_specs=(P("dp", "mp"), P("dp"), P("mp")),
        check_vma=False,
    )
```
